128 devices in a mesh: outer: 16 (over y_lo, z, core), inner: 8 (over x, y_hi).
Axes of the slice: x: 4, y: 4 (y_hi: 2, y_lo: 2; y = y_hi * 2 + y_lo), z: 4, core: 2. Of those that a mesh axis runs over, the one named last changes fastest.
Arguments:
- query_rows: bfloat16 [16384, 1024], P(('outer', 'inner')), may hold values from -8 to 8
- key_rows: bfloat16 [16384, 128], P(('outer', 'inner')), may hold values from -6 to 6
- value_rows: bfloat16 [16384, 128], P(('outer', 'inner')), may hold values from -0.59765625 to 0.59765625
- saved_output: bfloat16 [16384, 1024], P(('outer', 'inner')), may hold values from -0.59765625 to 0.59765625
- output_grad: bfloat16 [16384, 1024], P(('outer', 'inner')), may hold values from -6 to 6
- logsumexp: float32 [8, 16384], P(None, ('outer', 'inner')), as said below
- block_order: int32 [256], replicated, may hold values from 0 to 255, as said below
Outputs:
- query_grad: bfloat16 [16384, 1024], P(('outer', 'inner'))
- key_grad: bfloat16 [16384, 128], P(('outer', 'inner'))
- value_grad: bfloat16 [16384, 128], P(('outer', 'inner'))
The draws below stay inside these ranges and needn't reach their ends.
Inputs may be any that keep to these rules, and one draw needn't show every extreme that they name: `block_order`: each number from 0 to 255 appears once. `logsumexp`: close to the log of the softmax total of the query at that position.
All inputs are finite; a program needn't handle non-finite values.
Results may differ from the reference program's by a relative error of at most 0.005.
Values may be sent and summed in bfloat16 or wider, within the bound.
No kernel may reach another device: no remote copies, remote signals or barrier semaphores. Data moves between devices by JAX's collectives and lax.ppermute only.
A program may use at most 128 MiB of HBM per device.

```python
import math
import jax
import jax.numpy as jnp
from jax import lax

HEAD = 128
HEADS = 8
BLOCK = 64
SEQ = 16384


def shared_order(key):
    return jax.random.permutation(key, SEQ // BLOCK).astype(jnp.int32)


def draw_block_order(key, part):
    return shared_order(key)


def draw_logsumexp(key, part):
    listing = shared_order(key)
    key = jax.random.fold_in(key, 7)
    positions = (listing[:, None] * BLOCK + jnp.arange(BLOCK, dtype=jnp.int32)[None, :]).reshape(-1)
    spread = jax.random.uniform(key, (HEADS, SEQ), jnp.float32, -0.5, 0.5)
    return jnp.log(positions.astype(jnp.float32)[None, :] + 1.0) + 1.1 + spread


def block_scale(rng, shape, split, smallest, top_value):
    factor_of, own = 1.0, jax.random.fold_in(rng, 6)
    for axis_at, parts in split:
        heights = jnp.exp(jax.random.uniform(jax.random.fold_in(own, axis_at), (parts,), jnp.float32, smallest / len(split), top_value / len(split)))
        factor_of = factor_of * jnp.repeat(heights, shape[axis_at] // parts).reshape([-1 if axis == axis_at else 1 for axis in range(len(shape))])
    return factor_of


def centred(own_key, extent, scale, limit, shards=(), held_as=jnp.bfloat16):
    drawn = scale * jax.random.normal(own_key, extent, jnp.float32)
    if shards:
        drawn = drawn * block_scale(own_key, extent, shards, -0.22, 0.18)
    return jnp.clip(drawn, -limit, limit).astype(held_as)


def setup_inputs(seed: int = 0) -> dict:
    key_of = jax.random.split(jax.random.key(seed), 8)
    query_rows = centred(key_of[0], (SEQ, HEADS * HEAD), 1.5, 8.0, ((0, 128),))
    key_rows = centred(key_of[1], (SEQ, HEAD), 1.0, 6.0, ((0, 128),))
    value_rows = centred(key_of[2], (SEQ, HEAD), 0.1, 0.59765625, ((0, 128),))
    saved_output = centred(key_of[3], (SEQ, HEADS * HEAD), 0.1, 0.59765625, ((0, 128),))
    output_grad = centred(key_of[4], (SEQ, HEADS * HEAD), 1.0, 6.0, ((0, 128),))
    logsumexp = draw_logsumexp(jax.random.fold_in(key_of[7], 71), 0)
    block_order = draw_block_order(jax.random.fold_in(key_of[7], 71), 0)
    return {"query_rows": query_rows, "key_rows": key_rows, "value_rows": value_rows, "saved_output": saved_output, "output_grad": output_grad, "logsumexp": logsumexp, "block_order": block_order}


def reference(query_rows, key_rows, value_rows, saved_output, output_grad, logsumexp, block_order):
    scale = 1.0 / math.sqrt(HEAD)
    positions = (block_order[:, None] * BLOCK + jnp.arange(BLOCK, dtype=jnp.int32)[None, :]).reshape(-1).astype(jnp.int32)
    query_heads = query_rows.reshape(SEQ, HEADS, HEAD).astype(jnp.float32)
    grad_heads = output_grad.reshape(SEQ, HEADS, HEAD).astype(jnp.float32)
    saved_heads = saved_output.reshape(SEQ, HEADS, HEAD).astype(jnp.float32)
    deltas = lax.optimization_barrier(jnp.sum(grad_heads * saved_heads, axis=2)).T
    key_full = key_rows.astype(jnp.float32)
    value_full = value_rows.astype(jnp.float32)
    span = math.gcd(SEQ, 512)

    def step(carry, index):
        key_acc, value_acc = carry
        start = (index * span).astype(jnp.int32)
        query_blk = lax.dynamic_slice_in_dim(query_heads, start, span, 0)
        grad_blk = lax.dynamic_slice_in_dim(grad_heads, start, span, 0)
        pos_blk = lax.dynamic_slice_in_dim(positions, start, span, 0)
        lse_blk = lax.dynamic_slice_in_dim(logsumexp, start, span, 1)
        delta_blk = lax.dynamic_slice_in_dim(deltas, start, span, 1)
        scores = jnp.einsum('thd,kd->htk', query_blk, key_full) * scale
        allowed = pos_blk[None, :, None] >= positions[None, None, :]
        probs = jnp.where(allowed, jnp.exp(scores - lse_blk[:, :, None]), 0.0)
        dprobs = jnp.einsum('thd,kd->htk', grad_blk, value_full)
        dscores = probs * (dprobs - delta_blk[:, :, None])
        probs_half = lax.optimization_barrier(probs.astype(jnp.bfloat16)).astype(jnp.float32)
        dscores_half = lax.optimization_barrier(dscores.astype(jnp.bfloat16)).astype(jnp.float32)
        value_add = jnp.einsum('htk,thd->kd', probs_half, grad_blk)
        key_add = jnp.einsum('htk,thd->kd', dscores_half, query_blk) * scale
        query_add = jnp.einsum('htk,kd->thd', dscores_half, key_full) * scale
        return ((key_acc + key_add, value_acc + value_add), query_add.astype(jnp.bfloat16))
    start_acc = (jnp.zeros((SEQ, HEAD), jnp.float32), jnp.zeros((SEQ, HEAD), jnp.float32))
    (key_acc, value_acc), query_parts = lax.scan(step, start_acc, jnp.arange(SEQ // span, dtype=jnp.int32))
    query_grad = query_parts.reshape(SEQ, HEADS * HEAD)
    return (query_grad, key_acc.astype(jnp.bfloat16), value_acc.astype(jnp.bfloat16))
```

```python
import functools
import math

import jax
import jax.numpy as jnp
from jax import lax
from jax.experimental import pallas as pl
from jax.experimental.pallas import tpu as pltpu
from jax.sharding import PartitionSpec as P

WIDTH = 128
BLOCK = 64
KEY_TILE = 512
PAIR = 2
HALF_HEADS = 4
COLS = HALF_HEADS * BLOCK
LOG2E = 1.4426950408889634
AXES = ("outer", "inner")


def linear(x, y, z, core):
    return (((y % 2) * 4 + z) * 2 + core) * 8 + x * 2 + y // 2


def place(index):
    inner = index % 8
    outer = index // 8
    return inner // 2, (inner % 2) * 2 + outer // 8, (outer // 2) % 4, outer % 2


def shift(block, dx=0, dy=0, dz=0, dcore=0):
    route = []
    for index in range(128):
        x, y, z, core = place(index)
        to = linear((x + dx) % 4, (y + dy) % 4, (z + dz) % 4, (core + dcore) % 2)
        route.append((index, to))
    return lax.ppermute(block, AXES, route)


def nt(a, b):
    return lax.dot_general(a, b, (((1,), (1,)), ((), ())), preferred_element_type=jnp.float32)


def nn(a, b):
    return lax.dot_general(a, b, (((1,), (0,)), ((), ())), preferred_element_type=jnp.float32)


def attend_kernel(
    q_rank, k_rank, q_sorted, k_sorted,
    pay0, pay1, pay2, pay3, st0, st1, st2, st3, kv_own, kv_sib,
    dq0, dq1, dq2, dq3, dkv_own, dkv_sib,
    ks, vs, kt, dk, dv, qs, gs, dq, lse_s, del_s, s_scr, p_scr, ti, tj,
):
    pays, stats, dqs = (pay0, pay1, pay2, pay3), (st0, st1, st2, st3), (dq0, dq1, dq2, dq3)
    key_blocks, query_blocks = k_rank.shape[0], q_rank.shape[0]
    per_tile = KEY_TILE // BLOCK
    key_tiles, query_tiles = key_blocks // per_tile, query_blocks // PAIR
    half_keys = key_blocks // 2
    span = PAIR * COLS
    scale = 1.0 / math.sqrt(WIDTH)
    factor = scale * LOG2E

    for half, kv in enumerate((kv_own, kv_sib)):
        def bring(r, _, kv=kv, half=half):
            src = pl.multiple_of(r * BLOCK, BLOCK)
            dst = pl.multiple_of(k_rank[half * half_keys + r] * BLOCK, BLOCK)
            ks[pl.ds(dst, BLOCK), :] = kv[pl.ds(src, BLOCK), :WIDTH]
            vs[pl.ds(dst, BLOCK), :] = kv[pl.ds(src, BLOCK), WIDTH:]
            return 0
        lax.fori_loop(0, half_keys, bring, 0, unroll=4)

    def ready(j, _):
        kt[j] = ks[pl.ds(pl.multiple_of(j * KEY_TILE, KEY_TILE), KEY_TILE), :].T
        dk[j] = jnp.zeros((KEY_TILE, WIDTH), jnp.float32)
        dv[j] = jnp.zeros((KEY_TILE, WIDTH), jnp.float32)
        return 0
    lax.fori_loop(0, key_tiles, ready, 0)

    for s in range(query_blocks):
        pay, stat, rows = pays[s // 4], stats[s // 4], (s % 4) * BLOCK
        rank = q_rank[s]
        dst = pl.multiple_of(rank * COLS, COLS)
        for h in range(HALF_HEADS):
            qs[pl.ds(dst + h * BLOCK, BLOCK), :] = pay[rows:rows + BLOCK, h * WIDTH:(h + 1) * WIDTH]
            gs[pl.ds(dst + h * BLOCK, BLOCK), :] = pay[
                rows:rows + BLOCK, (HALF_HEADS + h) * WIDTH:(HALF_HEADS + h + 1) * WIDTH]
        top, lanes = (s % 4) // 2 * 8, slice((s % 2) * BLOCK, (s % 2 + 1) * BLOCK)
        lse_s[pl.ds(rank, 1), :] = jnp.concatenate(
            [stat[top + h:top + h + 1, lanes] for h in range(HALF_HEADS)], axis=1) * LOG2E
        del_s[pl.ds(rank, 1), :] = jnp.concatenate(
            [stat[top + HALF_HEADS + h:top + HALF_HEADS + h + 1, lanes] for h in range(HALF_HEADS)],
            axis=1)

    def listing(i, carry):
        n, total = carry
        dq[i] = jnp.zeros((WIDTH, span), jnp.float32)
        top = q_sorted[i * PAIR + PAIR - 1]
        n = lax.while_loop(
            lambda n: (n < key_blocks) & (k_sorted[jnp.minimum(n, key_blocks - 1)] <= top),
            lambda n: n + 1, n)
        def put(j, total):
            ti[total] = i
            tj[total] = j
            return total + 1
        return n, lax.fori_loop(0, (n + per_tile - 1) // per_tile, put, total)
    _, total = lax.fori_loop(0, query_tiles, listing, (jnp.int32(0), jnp.int32(0)))
    for extra in range(2):
        ti[total + extra] = 0
        tj[total + extra] = 0

    in_query = lax.broadcasted_iota(jnp.int32, (1, span), 1) % BLOCK
    in_key = lax.broadcasted_iota(jnp.int32, (BLOCK, span), 0)

    def front(t, slot):
        i, j = ti[t], tj[t]
        ko, qo = pl.multiple_of(j * KEY_TILE, KEY_TILE), pl.multiple_of(i * span, span)
        s_scr[slot] = nt(ks[pl.ds(ko, KEY_TILE), :], qs[pl.ds(qo, span), :])
        p_scr[slot] = nt(vs[pl.ds(ko, KEY_TILE), :], gs[pl.ds(qo, span), :])

    def back(t, slot):
        i, j = ti[t], tj[t]
        live = t < total
        qo = pl.multiple_of(i * span, span)
        lse = jnp.concatenate([lse_s[pl.ds(i * PAIR + u, 1), :] for u in range(PAIR)], axis=1)
        delta = jnp.concatenate([del_s[pl.ds(i * PAIR + u, 1), :] for u in range(PAIR)], axis=1)
        query_pos = in_query + jnp.concatenate(
            [jnp.full((1, COLS), jnp.where(live, q_sorted[i * PAIR + u] * BLOCK, -BLOCK), jnp.int32)
             for u in range(PAIR)], axis=1)
        probs_parts, dscores_parts = [], []
        for u in range(per_tile):
            scores = s_scr[slot, u * BLOCK:(u + 1) * BLOCK, :]
            dprobs = p_scr[slot, u * BLOCK:(u + 1) * BLOCK, :]
            allowed = in_key <= query_pos - k_sorted[j * per_tile + u] * BLOCK
            probs = jnp.where(allowed, jnp.exp2(scores * factor - lse), 0.0)
            dscores_parts.append((probs * (dprobs - delta)).astype(jnp.bfloat16))
            probs_parts.append(probs.astype(jnp.bfloat16))
        probs_half = jnp.concatenate(probs_parts, axis=0)
        dscores_half = jnp.concatenate(dscores_parts, axis=0)
        dv[j] += nn(probs_half, gs[pl.ds(qo, span), :])
        dk[j] += nn(dscores_half, qs[pl.ds(qo, span), :])
        dq[i] += nn(kt[j], dscores_half)

    front(0, 0)

    def two(h, _):
        front(2 * h + 1, 1)
        back(2 * h, 0)
        front(2 * h + 2, 0)
        back(2 * h + 1, 1)
        return 0
    lax.fori_loop(0, (total + 1) // 2, two, 0)

    def turn(i, _):
        rows = (dq[i].T * scale).astype(jnp.bfloat16)
        qs[pl.ds(pl.multiple_of(i * span, span), span), :] = rows
        return 0
    lax.fori_loop(0, query_tiles, turn, 0)
    for s in range(query_blocks):
        src = pl.multiple_of(q_rank[s] * COLS, COLS)
        rows = (s % 4) * BLOCK
        for h in range(HALF_HEADS):
            dqs[s // 4][rows:rows + BLOCK, h * WIDTH:(h + 1) * WIDTH] = qs[
                pl.ds(src + h * BLOCK, BLOCK), :]
    for half, out in enumerate((dkv_own, dkv_sib)):
        def give(r, _, out=out, half=half):
            dst = pl.multiple_of(r * BLOCK, BLOCK)
            rank = k_rank[half * half_keys + r]
            j, src = rank // per_tile, pl.multiple_of(rank % per_tile * BLOCK, BLOCK)
            out[pl.ds(dst, BLOCK), :WIDTH] = (dk[j, pl.ds(src, BLOCK), :] * scale).astype(jnp.bfloat16)
            out[pl.ds(dst, BLOCK), WIDTH:] = dv[j, pl.ds(src, BLOCK), :].astype(jnp.bfloat16)
            return 0
        lax.fori_loop(0, half_keys, give, 0, unroll=4)


def attend(q_rank, k_rank, q_sorted, k_sorted, pays, stats, kv_own, kv_sib):
    key_blocks, query_blocks = k_rank.shape[0], q_rank.shape[0]
    keys = key_blocks * BLOCK
    key_tiles, query_tiles = keys // KEY_TILE, query_blocks // PAIR
    span = PAIR * COLS
    bf16, f32 = jnp.bfloat16, jnp.float32
    smem, vmem = pl.BlockSpec(memory_space=pltpu.SMEM), pl.BlockSpec(memory_space=pltpu.VMEM)
    listed = query_tiles * key_tiles + 2
    return pl.pallas_call(
        attend_kernel,
        in_specs=[smem] * 4 + [vmem] * 10,
        out_specs=[vmem] * 6,
        out_shape=[jax.ShapeDtypeStruct((4 * BLOCK, HALF_HEADS * WIDTH), bf16)] * 4
        + [jax.ShapeDtypeStruct((keys // 2, 2 * WIDTH), bf16)] * 2,
        scratch_shapes=[
            pltpu.VMEM((keys, WIDTH), bf16),
            pltpu.VMEM((keys, WIDTH), bf16),
            pltpu.VMEM((key_tiles, WIDTH, KEY_TILE), bf16),
            pltpu.VMEM((key_tiles, KEY_TILE, WIDTH), f32),
            pltpu.VMEM((key_tiles, KEY_TILE, WIDTH), f32),
            pltpu.VMEM((query_blocks * COLS, WIDTH), bf16),
            pltpu.VMEM((query_blocks * COLS, WIDTH), bf16),
            pltpu.VMEM((query_tiles, WIDTH, span), f32),
            pltpu.VMEM((query_blocks, COLS), f32),
            pltpu.VMEM((query_blocks, COLS), f32),
            pltpu.VMEM((2, KEY_TILE, span), f32),
            pltpu.VMEM((2, KEY_TILE, span), f32),
            pltpu.SMEM((listed,), jnp.int32),
            pltpu.SMEM((listed,), jnp.int32),
        ],
        compiler_params=pltpu.CompilerParams(vmem_limit_bytes=48 * 1024 * 1024),
    )(q_rank, k_rank, q_sorted, k_sorted, *pays, *stats, kv_own, kv_sib)


def ranked(block_order, blocks):
    listed = jnp.arange(block_order.shape[0], dtype=jnp.int32)
    pos = jnp.sum(jnp.where(blocks[:, None] == listed[None, :], block_order[None, :], 0), axis=1)
    rank = jnp.sum((pos[None, :] < pos[:, None]).astype(jnp.int32), axis=1)
    at = jnp.arange(blocks.shape[0], dtype=jnp.int32)
    return rank, jnp.sum(jnp.where(rank[None, :] == at[:, None], pos[None, :], 0), axis=1)


def total_of(parts):
    return functools.reduce(lambda a, b: a + b, [p.astype(jnp.float32) for p in parts])


def body(query_rows, key_rows, value_rows, saved_output, output_grad, logsumexp, block_order):
    rows = query_rows.shape[0]
    half = HALF_HEADS * WIDTH
    x, y, z, core = place(lax.axis_index("outer") * 8 + lax.axis_index("inner"))
    first = core == 0

    def mine(array):
        return jnp.where(first, array[:, :half], array[:, half:])

    def other(array):
        return jnp.where(first, array[:, half:], array[:, :half])

    kv = jnp.concatenate([key_rows, value_rows], axis=1)
    kv_line = jnp.concatenate([kv] + [shift(kv, dz=-d) for d in (1, 2, 3)], axis=0)
    sib = shift(jnp.concatenate([other(query_rows), other(output_grad)], axis=1), dcore=1)
    pay = jnp.concatenate(
        [jnp.concatenate([mine(query_rows), mine(output_grad)], axis=1), sib], axis=0)
    pays = [pay] + [shift(pay, dy=-d) for d in (1, 2, 3)]
    kv_own = jnp.concatenate([kv_line] + [shift(kv_line, dx=-d) for d in (1, 2, 3)], axis=0)
    kv_sib = shift(kv_own, dcore=1)

    heads = (rows, 2 * HALF_HEADS, WIDTH)
    delta = jnp.sum(
        output_grad.reshape(heads).astype(jnp.float32)
        * saved_output.reshape(heads).astype(jnp.float32), axis=2).T
    low = jnp.concatenate([logsumexp[:HALF_HEADS], delta[:HALF_HEADS]], axis=0)
    high = jnp.concatenate([logsumexp[HALF_HEADS:], delta[HALF_HEADS:]], axis=0)
    stat = jnp.concatenate(
        [jnp.where(first, low, high), shift(jnp.where(first, high, low), dcore=1)], axis=0)
    stats = [stat] + [shift(stat, dy=-d) for d in (1, 2, 3)]

    four = jnp.arange(4, dtype=jnp.int32)
    two = jnp.arange(2, dtype=jnp.int32)
    dy, cs, b = (a.reshape(-1) for a in jnp.meshgrid(four, two, two, indexing="ij"))
    q_rank, q_sorted = ranked(block_order, 2 * linear(x, (y + dy) % 4, z, (core + cs) % 2) + b)
    cs, dx, dz, b = (a.reshape(-1) for a in jnp.meshgrid(two, four, four, two, indexing="ij"))
    k_rank, k_sorted = ranked(
        block_order, 2 * linear((x + dx) % 4, y, (z + dz) % 4, (core + cs) % 2) + b)

    *dqs, dkv_own, dkv_sib = attend(
        q_rank, k_rank, q_sorted, k_sorted, pays, stats, kv_own, kv_sib)

    dkv = total_of([dkv_own, shift(dkv_sib, dcore=1)]).astype(jnp.bfloat16)
    dq = total_of([dqs[0]] + [shift(dqs[d], dy=d) for d in (1, 2, 3)]).astype(jnp.bfloat16)
    quarter = dkv.shape[0] // 4
    parts = [dkv[d * quarter:(d + 1) * quarter] for d in range(4)]
    line = total_of([parts[0]] + [shift(parts[d], dx=d) for d in (1, 2, 3)]).astype(jnp.bfloat16)
    parts = [line[d * rows:(d + 1) * rows] for d in range(4)]
    done = total_of([parts[0]] + [shift(parts[d], dz=d) for d in (1, 2, 3)])
    near, far = dq[:rows], shift(dq[rows:], dcore=1)
    query_grad = jnp.concatenate(
        [jnp.where(first, near, far), jnp.where(first, far, near)], axis=1)
    return (
        query_grad,
        done[:, :WIDTH].astype(jnp.bfloat16),
        done[:, WIDTH:].astype(jnp.bfloat16),
    )


def solution(mesh):
    rows = P(AXES, None)
    return jax.shard_map(
        body,
        mesh=mesh,
        in_specs=(rows, rows, rows, rows, rows, P(None, AXES), P()),
        out_specs=(rows, rows, rows),
        check_vma=False,
    )
```

```python
import functools
import math

import jax
import jax.numpy as jnp
from jax import lax
from jax.experimental import pallas as pl
from jax.experimental.pallas import tpu as pltpu
from jax.sharding import PartitionSpec as P

WIDTH = 128
BLOCK = 64
KEY_TILE = 512
PAIR = 2
HALF_HEADS = 4
COLS = HALF_HEADS * BLOCK
STAT_ROWS = 16
PAY_ROWS = 2 * BLOCK + STAT_ROWS
LOG2E = 1.4426950408889634
AXES = ("outer", "inner")


def linear(x, y, z, core):
    return (((y % 2) * 4 + z) * 2 + core) * 8 + x * 2 + y // 2


def place(index):
    inner = index % 8
    outer = index // 8
    return inner // 2, (inner % 2) * 2 + outer // 8, (outer // 2) % 4, outer % 2


def shift(block, dx=0, dy=0, dz=0, dcore=0):
    route = []
    for index in range(128):
        x, y, z, core = place(index)
        to = linear((x + dx) % 4, (y + dy) % 4, (z + dz) % 4, (core + dcore) % 2)
        route.append((index, to))
    return lax.ppermute(block, AXES, route)


def nt(a, b):
    return lax.dot_general(a, b, (((1,), (1,)), ((), ())), preferred_element_type=jnp.float32)


def nn(a, b):
    return lax.dot_general(a, b, (((1,), (0,)), ((), ())), preferred_element_type=jnp.float32)


def attend_kernel(
    q_rank, k_rank, q_sorted, k_sorted,
    pay0, pay1, pay2a, pay2b, pay3, kv_own, kv_sib,
    dq_own, dq_sib, dkv_own, dkv_sib,
    ks, vs, kt, dk, dv, qs, gs, dq, lse_s, del_s, s_scr, p_scr, ti, tj,
):
    key_blocks, query_blocks = k_rank.shape[0], q_rank.shape[0]
    per_tile = KEY_TILE // BLOCK
    key_tiles, query_tiles = key_blocks // per_tile, query_blocks // PAIR
    half_keys = key_blocks // 2
    span = PAIR * COLS
    scale = 1.0 / math.sqrt(WIDTH)
    factor = scale * LOG2E

    for half, kv in enumerate((kv_own, kv_sib)):
        def bring(r, _, kv=kv, half=half):
            src = pl.multiple_of(r * BLOCK, BLOCK)
            dst = pl.multiple_of(k_rank[half * half_keys + r] * BLOCK, BLOCK)
            ks[pl.ds(dst, BLOCK), :] = kv[pl.ds(src, BLOCK), :WIDTH]
            vs[pl.ds(dst, BLOCK), :] = kv[pl.ds(src, BLOCK), WIDTH:]
            return 0
        lax.fori_loop(0, half_keys, bring, 0, unroll=4)

    def ready(j, _):
        kt[j] = ks[pl.ds(pl.multiple_of(j * KEY_TILE, KEY_TILE), KEY_TILE), :].T
        dk[j] = jnp.zeros((KEY_TILE, WIDTH), jnp.float32)
        dv[j] = jnp.zeros((KEY_TILE, WIDTH), jnp.float32)
        return 0
    lax.fori_loop(0, key_tiles, ready, 0)

    for s in range(query_blocks):
        pay, own = ((pay0, pay1, pay2a, pay3)[s // 4], s % 4 // 2 * PAY_ROWS)
        if s // 4 == 2:
            pay, own = (pay2a, pay2b)[s % 4 // 2], 0
        rows = own + s % 2 * BLOCK
        rank = q_rank[s]
        dst = pl.multiple_of(rank * COLS, COLS)
        for h in range(HALF_HEADS):
            qs[pl.ds(dst + h * BLOCK, BLOCK), :] = pay[rows:rows + BLOCK, h * WIDTH:(h + 1) * WIDTH]
            gs[pl.ds(dst + h * BLOCK, BLOCK), :] = pay[
                rows:rows + BLOCK, (HALF_HEADS + h) * WIDTH:(HALF_HEADS + h + 1) * WIDTH]
        stat = sum(
            pay[own + PAY_ROWS - STAT_ROWS:own + PAY_ROWS, n * WIDTH:(n + 1) * WIDTH].astype(jnp.float32)
            for n in range(3))
        lanes = slice(s % 2 * BLOCK, (s % 2 + 1) * BLOCK)
        lse_s[pl.ds(rank, 1), :] = jnp.concatenate(
            [stat[h:h + 1, lanes] for h in range(HALF_HEADS)], axis=1) * LOG2E
        del_s[pl.ds(rank, 1), :] = jnp.concatenate(
            [stat[HALF_HEADS + h:HALF_HEADS + h + 1, lanes] for h in range(HALF_HEADS)], axis=1)

    def listing(i, carry):
        n, total = carry
        dq[i] = jnp.zeros((WIDTH, span), jnp.float32)
        top = q_sorted[i * PAIR + PAIR - 1]
        n = lax.while_loop(
            lambda n: (n < key_blocks) & (k_sorted[jnp.minimum(n, key_blocks - 1)] <= top),
            lambda n: n + 1, n)
        def put(j, total):
            ti[total] = i
            tj[total] = j
            return total + 1
        return n, lax.fori_loop(0, (n + per_tile - 1) // per_tile, put, total)
    _, total = lax.fori_loop(0, query_tiles, listing, (jnp.int32(0), jnp.int32(0)))
    for extra in range(2):
        ti[total + extra] = 0
        tj[total + extra] = 0

    in_query = lax.broadcasted_iota(jnp.int32, (1, span), 1) % BLOCK
    in_key = lax.broadcasted_iota(jnp.int32, (BLOCK, span), 0)

    def front(t, slot):
        i, j = ti[t], tj[t]
        ko, qo = pl.multiple_of(j * KEY_TILE, KEY_TILE), pl.multiple_of(i * span, span)
        s_scr[slot] = nt(ks[pl.ds(ko, KEY_TILE), :], qs[pl.ds(qo, span), :])
        p_scr[slot] = nt(vs[pl.ds(ko, KEY_TILE), :], gs[pl.ds(qo, span), :])

    def back(t, slot):
        i, j = ti[t], tj[t]
        live = t < total
        qo = pl.multiple_of(i * span, span)
        lse = jnp.concatenate([lse_s[pl.ds(i * PAIR + u, 1), :] for u in range(PAIR)], axis=1)
        delta = jnp.concatenate([del_s[pl.ds(i * PAIR + u, 1), :] for u in range(PAIR)], axis=1)
        query_pos = in_query + jnp.concatenate(
            [jnp.full((1, COLS), jnp.where(live, q_sorted[i * PAIR + u] * BLOCK, -BLOCK), jnp.int32)
             for u in range(PAIR)], axis=1)
        probs_parts, dscores_parts = [], []
        for u in range(per_tile):
            scores = s_scr[slot, u * BLOCK:(u + 1) * BLOCK, :]
            dprobs = p_scr[slot, u * BLOCK:(u + 1) * BLOCK, :]
            allowed = in_key <= query_pos - k_sorted[j * per_tile + u] * BLOCK
            probs = jnp.where(allowed, jnp.exp2(scores * factor - lse), 0.0)
            dscores_parts.append((probs * (dprobs - delta)).astype(jnp.bfloat16))
            probs_parts.append(probs.astype(jnp.bfloat16))
        probs_half = jnp.concatenate(probs_parts, axis=0)
        dscores_half = jnp.concatenate(dscores_parts, axis=0)
        dv[j] += nn(probs_half, gs[pl.ds(qo, span), :])
        dk[j] += nn(dscores_half, qs[pl.ds(qo, span), :])
        dq[i] += nn(kt[j], dscores_half)

    front(0, 0)

    def two(h, _):
        front(2 * h + 1, 1)
        back(2 * h, 0)
        front(2 * h + 2, 0)
        back(2 * h + 1, 1)
        return 0
    lax.fori_loop(0, (total + 1) // 2, two, 0)

    def turn(i, _):
        rows = (dq[i].T * scale).astype(jnp.bfloat16)
        qs[pl.ds(pl.multiple_of(i * span, span), span), :] = rows
        return 0
    lax.fori_loop(0, query_tiles, turn, 0)
    for s in range(query_blocks):
        src = pl.multiple_of(q_rank[s] * COLS, COLS)
        out = (dq_own, dq_sib)[s % 4 // 2]
        rows = s // 4 * 2 * BLOCK + s % 2 * BLOCK
        for h in range(HALF_HEADS):
            out[rows:rows + BLOCK, h * WIDTH:(h + 1) * WIDTH] = qs[
                pl.ds(src + h * BLOCK, BLOCK), :]
    for half, out in enumerate((dkv_own, dkv_sib)):
        def give(r, _, out=out, half=half):
            dst = pl.multiple_of(r * BLOCK, BLOCK)
            rank = k_rank[half * half_keys + r]
            j, src = rank // per_tile, pl.multiple_of(rank % per_tile * BLOCK, BLOCK)
            out[pl.ds(dst, BLOCK), :WIDTH] = (dk[j, pl.ds(src, BLOCK), :] * scale).astype(jnp.bfloat16)
            out[pl.ds(dst, BLOCK), WIDTH:] = dv[j, pl.ds(src, BLOCK), :].astype(jnp.bfloat16)
            return 0
        lax.fori_loop(0, half_keys, give, 0, unroll=4)


def attend(q_rank, k_rank, q_sorted, k_sorted, pays, kv_own, kv_sib):
    key_blocks, query_blocks = k_rank.shape[0], q_rank.shape[0]
    keys = key_blocks * BLOCK
    key_tiles, query_tiles = keys // KEY_TILE, query_blocks // PAIR
    span = PAIR * COLS
    bf16, f32 = jnp.bfloat16, jnp.float32
    smem, vmem = pl.BlockSpec(memory_space=pltpu.SMEM), pl.BlockSpec(memory_space=pltpu.VMEM)
    listed = query_tiles * key_tiles + 2
    return pl.pallas_call(
        attend_kernel,
        in_specs=[smem] * 4 + [vmem] * 7,
        out_specs=[vmem] * 4,
        out_shape=[jax.ShapeDtypeStruct((8 * BLOCK, HALF_HEADS * WIDTH), bf16)] * 2
        + [jax.ShapeDtypeStruct((keys // 2, 2 * WIDTH), bf16)] * 2,
        scratch_shapes=[
            pltpu.VMEM((keys, WIDTH), bf16),
            pltpu.VMEM((keys, WIDTH), bf16),
            pltpu.VMEM((key_tiles, WIDTH, KEY_TILE), bf16),
            pltpu.VMEM((key_tiles, KEY_TILE, WIDTH), f32),
            pltpu.VMEM((key_tiles, KEY_TILE, WIDTH), f32),
            pltpu.VMEM((query_blocks * COLS, WIDTH), bf16),
            pltpu.VMEM((query_blocks * COLS, WIDTH), bf16),
            pltpu.VMEM((query_tiles, WIDTH, span), f32),
            pltpu.VMEM((query_blocks, COLS), f32),
            pltpu.VMEM((query_blocks, COLS), f32),
            pltpu.VMEM((2, KEY_TILE, span), f32),
            pltpu.VMEM((2, KEY_TILE, span), f32),
            pltpu.SMEM((listed,), jnp.int32),
            pltpu.SMEM((listed,), jnp.int32),
        ],
        compiler_params=pltpu.CompilerParams(vmem_limit_bytes=48 * 1024 * 1024),
    )(q_rank, k_rank, q_sorted, k_sorted, *pays, kv_own, kv_sib)


def ranked(block_order, blocks):
    listed = jnp.arange(block_order.shape[0], dtype=jnp.int32)
    pos = jnp.sum(jnp.where(blocks[:, None] == listed[None, :], block_order[None, :], 0), axis=1)
    rank = jnp.sum((pos[None, :] < pos[:, None]).astype(jnp.int32), axis=1)
    at = jnp.arange(blocks.shape[0], dtype=jnp.int32)
    return rank, jnp.sum(jnp.where(rank[None, :] == at[:, None], pos[None, :], 0), axis=1)


def total_of(parts):
    return functools.reduce(lambda a, b: a + b, [p.astype(jnp.float32) for p in parts])


def thirds(array):
    high = lax.reduce_precision(array, 8, 7)
    middle = lax.reduce_precision(array - high, 8, 7)
    low = lax.reduce_precision(array - high - middle, 8, 7)
    return jnp.concatenate([high, middle, low], axis=1).astype(jnp.bfloat16)


def body(query_rows, key_rows, value_rows, saved_output, output_grad, logsumexp, block_order):
    rows = query_rows.shape[0]
    half = HALF_HEADS * WIDTH
    x, y, z, core = place(lax.axis_index("outer") * 8 + lax.axis_index("inner"))
    first = core == 0

    def mine(array):
        return jnp.where(first, array[:, :half], array[:, half:])

    def other(array):
        return jnp.where(first, array[:, half:], array[:, :half])

    heads = (rows, 2 * HALF_HEADS, WIDTH)
    delta = jnp.sum(
        output_grad.reshape(heads).astype(jnp.float32)
        * saved_output.reshape(heads).astype(jnp.float32), axis=2).T
    low = thirds(jnp.concatenate([logsumexp[:HALF_HEADS], delta[:HALF_HEADS]], axis=0))
    high = thirds(jnp.concatenate([logsumexp[HALF_HEADS:], delta[HALF_HEADS:]], axis=0))

    def packed(side, stat):
        stat = jnp.pad(stat, ((0, STAT_ROWS - stat.shape[0]), (0, 2 * half - stat.shape[1])))
        return jnp.concatenate(
            [jnp.concatenate([side(query_rows), side(output_grad)], axis=1), stat], axis=0)

    kv = jnp.concatenate([key_rows, value_rows], axis=1)
    sib = shift(packed(other, jnp.where(first, high, low)), dcore=1)
    pay = jnp.concatenate([packed(mine, jnp.where(first, low, high)), sib], axis=0)
    after, before = shift(pay, dy=-1), shift(pay, dy=1)
    kv_line = jnp.concatenate([kv] + [shift(kv, dz=-d) for d in (1, 2, 3)], axis=0)
    lines = [kv_line] + [shift(kv_line, dx=-d) for d in (1, 2, 3)]
    after, before, *lines = lax.optimization_barrier((after, before, *lines))
    kv_own = jnp.concatenate(lines, axis=0)
    kv_sib = shift(kv_own, dcore=1)
    across = shift(after[:PAY_ROWS], dy=-1), shift(before[PAY_ROWS:], dy=1)
    pays = [pay, after, *across, before]

    four = jnp.arange(4, dtype=jnp.int32)
    two = jnp.arange(2, dtype=jnp.int32)
    dy, cs, b = (a.reshape(-1) for a in jnp.meshgrid(four, two, two, indexing="ij"))
    q_rank, q_sorted = ranked(block_order, 2 * linear(x, (y + dy) % 4, z, (core + cs) % 2) + b)
    cs, dx, dz, b = (a.reshape(-1) for a in jnp.meshgrid(two, four, four, two, indexing="ij"))
    k_rank, k_sorted = ranked(
        block_order, 2 * linear((x + dx) % 4, y, (z + dz) % 4, (core + cs) % 2) + b)

    dq_own, dq_sib, dkv_own, dkv_sib = attend(
        q_rank, k_rank, q_sorted, k_sorted, pays, kv_own, kv_sib)

    dkv = total_of([dkv_own, shift(dkv_sib, dcore=1)]).astype(jnp.bfloat16)
    dq_far = shift(dq_sib, dcore=1)
    dq = jnp.concatenate(
        [jnp.where(first, dq_own, dq_far), jnp.where(first, dq_far, dq_own)], axis=1)
    quarter = dkv.shape[0] // 4
    parts = [dkv[d * quarter:(d + 1) * quarter] for d in range(4)]
    line = total_of([parts[0]] + [shift(parts[d], dx=d) for d in (1, 2, 3)]).astype(jnp.bfloat16)
    parts = [line[d * rows:(d + 1) * rows] for d in range(4)]
    done = total_of([parts[0]] + [shift(parts[d], dz=d) for d in (1, 2, 3)])
    parts = [dq[d * rows:(d + 1) * rows] for d in range(4)]
    query_grad = total_of([parts[0]] + [shift(parts[d], dy=d) for d in (1, 2, 3)]).astype(jnp.bfloat16)
    return (
        query_grad,
        done[:, :WIDTH].astype(jnp.bfloat16),
        done[:, WIDTH:].astype(jnp.bfloat16),
    )


def solution(mesh):
    rows = P(AXES, None)
    return jax.shard_map(
        body,
        mesh=mesh,
        in_specs=(rows, rows, rows, rows, rows, P(None, AXES), P()),
        out_specs=(rows, rows, rows),
        check_vma=False,
    )
```

```python
import functools
import math

import jax
import jax.numpy as jnp
from jax import lax
from jax.experimental import pallas as pl
from jax.experimental.pallas import tpu as pltpu
from jax.sharding import PartitionSpec as P

WIDTH = 128
BLOCK = 64
KEY_TILE = 512
PAIR = 2
HALF_HEADS = 4
COLS = HALF_HEADS * BLOCK
STAT_ROWS = 16
SIB_AT = 2 * BLOCK + STAT_ROWS
LOG2E = 1.4426950408889634
AXES = ("outer", "inner")


def linear(x, y, z, core):
    return (((y % 2) * 4 + z) * 2 + core) * 8 + x * 2 + y // 2


def place(index):
    inner = index % 8
    outer = index // 8
    return inner // 2, (inner % 2) * 2 + outer // 8, (outer // 2) % 4, outer % 2


def shift(block, dx=0, dy=0, dz=0, dcore=0):
    route = []
    for index in range(128):
        x, y, z, core = place(index)
        to = linear((x + dx) % 4, (y + dy) % 4, (z + dz) % 4, (core + dcore) % 2)
        route.append((index, to))
    return lax.ppermute(block, AXES, route)


def nt(a, b):
    return lax.dot_general(a, b, (((1,), (1,)), ((), ())), preferred_element_type=jnp.float32)


def nn(a, b):
    return lax.dot_general(a, b, (((1,), (0,)), ((), ())), preferred_element_type=jnp.float32)


def attend_kernel(
    q_rank, k_rank, q_sorted, k_sorted, counts,
    pay0, pay1, pay2a, pay2b, pay3, own0, own1, own2, own3, sib0, sib1, sib2,
    dq_own, dq_sib, dkv_own, dkv_sib,
    ks, vs, kt, dk, dv, qs, gs, dq, lse_s, del_s, s_scr, p_scr, plain, edge,
):
    key_blocks, query_blocks = k_rank.shape[0], q_rank.shape[0]
    per_tile = KEY_TILE // BLOCK
    key_tiles, query_tiles = key_blocks // per_tile, query_blocks // PAIR
    half_keys = key_blocks // 2
    span = PAIR * COLS
    scale = 1.0 / math.sqrt(WIDTH)
    factor = scale * LOG2E

    listed = 0
    for kv in (own0, own1, own2, own3, sib0, sib1, sib2):
        def bring(r, _, kv=kv, listed=listed):
            src = pl.multiple_of(r * BLOCK, BLOCK)
            dst = pl.multiple_of(k_rank[listed + r] * BLOCK, BLOCK)
            ks[pl.ds(dst, BLOCK), :] = kv[pl.ds(src, BLOCK), :WIDTH]
            vs[pl.ds(dst, BLOCK), :] = kv[pl.ds(src, BLOCK), WIDTH:]
            return 0
        lax.fori_loop(0, kv.shape[0] // BLOCK, bring, 0, unroll=4)
        listed += kv.shape[0] // BLOCK

    def ready(j, _):
        kt[j] = ks[pl.ds(pl.multiple_of(j * KEY_TILE, KEY_TILE), KEY_TILE), :].T
        dk[j] = jnp.zeros((KEY_TILE, WIDTH), jnp.float32)
        dv[j] = jnp.zeros((KEY_TILE, WIDTH), jnp.float32)
        return 0
    lax.fori_loop(0, key_tiles, ready, 0)

    for s in range(query_blocks):
        pay, side = (pay0, pay1, pay2a, pay3)[s // 4], s % 4 // 2
        stats, rows = pay, side * SIB_AT + s % 2 * BLOCK
        if s // 4 == 2 and side:
            pay, rows = pay2b, s % 2 * BLOCK
        rank = q_rank[s]
        dst = pl.multiple_of(rank * COLS, COLS)
        for h in range(HALF_HEADS):
            qs[pl.ds(dst + h * BLOCK, BLOCK), :] = pay[rows:rows + BLOCK, h * WIDTH:(h + 1) * WIDTH]
            gs[pl.ds(dst + h * BLOCK, BLOCK), :] = pay[
                rows:rows + BLOCK, (HALF_HEADS + h) * WIDTH:(HALF_HEADS + h + 1) * WIDTH]
        stat = sum(
            stats[2 * BLOCK:SIB_AT, n * WIDTH:(n + 1) * WIDTH].astype(jnp.float32)
            for n in range(3))
        top, lanes = side * 2 * HALF_HEADS, slice(s % 2 * BLOCK, (s % 2 + 1) * BLOCK)
        lse_s[pl.ds(rank, 1), :] = jnp.concatenate(
            [stat[top + h:top + h + 1, lanes] for h in range(HALF_HEADS)], axis=1) * LOG2E
        top += HALF_HEADS
        del_s[pl.ds(rank, 1), :] = jnp.concatenate(
            [stat[top + h:top + h + 1, lanes] for h in range(HALF_HEADS)], axis=1)

    def listing(i, carry):
        dq[i] = jnp.zeros((WIDTH, span), jnp.float32)

        def put(listed):
            def one(j, at):
                listed[0, at] = i
                listed[1, at] = j
                return at + 1
            return one
        plains, edges = carry
        plains = lax.fori_loop(0, counts[0, i], put(plain), plains)
        return plains, lax.fori_loop(counts[0, i], counts[1, i], put(edge), edges)
    plains, edges = lax.fori_loop(0, query_tiles, listing, (jnp.int32(0), jnp.int32(0)))
    for listed, total in ((plain, plains), (edge, edges)):
        for extra in range(2):
            listed[0, total + extra] = 0
            listed[1, total + extra] = 0

    in_query = lax.broadcasted_iota(jnp.int32, (1, span), 1) % BLOCK
    in_key = lax.broadcasted_iota(jnp.int32, (BLOCK, span), 0)

    def sweep(listed, total, masked):
        def front(t, slot):
            i, j = listed[0, t], listed[1, t]
            ko, qo = pl.multiple_of(j * KEY_TILE, KEY_TILE), pl.multiple_of(i * span, span)
            s_scr[slot] = nt(ks[pl.ds(ko, KEY_TILE), :], qs[pl.ds(qo, span), :])
            p_scr[slot] = nt(vs[pl.ds(ko, KEY_TILE), :], gs[pl.ds(qo, span), :])

        def back(t, slot):
            i, j = listed[0, t], listed[1, t]
            qo = pl.multiple_of(i * span, span)
            lse = jnp.concatenate([lse_s[pl.ds(i * PAIR + u, 1), :] for u in range(PAIR)], axis=1)
            lse = jnp.where(t < total, lse, 1e30)
            delta = jnp.concatenate([del_s[pl.ds(i * PAIR + u, 1), :] for u in range(PAIR)], axis=1)
            query_pos = in_query + jnp.concatenate(
                [jnp.full((1, COLS), q_sorted[i * PAIR + u] * BLOCK, jnp.int32) for u in range(PAIR)],
                axis=1)
            probs_parts, dscores_parts = [], []
            for u in range(per_tile):
                scores = s_scr[slot, u * BLOCK:(u + 1) * BLOCK, :]
                dprobs = p_scr[slot, u * BLOCK:(u + 1) * BLOCK, :]
                probs = jnp.exp2(scores * factor - lse)
                if masked:
                    allowed = in_key <= query_pos - k_sorted[j * per_tile + u] * BLOCK
                    probs = jnp.where(allowed, probs, 0.0)
                dscores_parts.append((probs * (dprobs - delta)).astype(jnp.bfloat16))
                probs_parts.append(probs.astype(jnp.bfloat16))
            probs_half = jnp.concatenate(probs_parts, axis=0)
            dscores_half = jnp.concatenate(dscores_parts, axis=0)
            dv[j] += nn(probs_half, gs[pl.ds(qo, span), :])
            dk[j] += nn(dscores_half, qs[pl.ds(qo, span), :])
            dq[i] += nn(kt[j], dscores_half)

        front(0, 0)

        def two(h, _):
            front(2 * h + 1, 1)
            back(2 * h, 0)
            front(2 * h + 2, 0)
            back(2 * h + 1, 1)
            return 0
        lax.fori_loop(0, (total + 1) // 2, two, 0)

    sweep(plain, plains, False)
    sweep(edge, edges, True)

    for s in range(query_blocks):
        rank = q_rank[s]
        out = (dq_own, dq_sib)[s % 4 // 2]
        rows = s // 4 * 2 * BLOCK + s % 2 * BLOCK
        block = dq[rank // PAIR, :, pl.ds(pl.multiple_of(rank % PAIR * COLS, COLS), COLS)]
        block = (block.T * scale).astype(jnp.bfloat16)
        for h in range(HALF_HEADS):
            out[rows:rows + BLOCK, h * WIDTH:(h + 1) * WIDTH] = block[h * BLOCK:(h + 1) * BLOCK]
    for half, out in enumerate((dkv_own, dkv_sib)):
        def give(r, _, out=out, half=half):
            dst = pl.multiple_of(r * BLOCK, BLOCK)
            rank = k_rank[half * half_keys + r]
            j, src = rank // per_tile, pl.multiple_of(rank % per_tile * BLOCK, BLOCK)
            out[pl.ds(dst, BLOCK), :WIDTH] = (dk[j, pl.ds(src, BLOCK), :] * scale).astype(jnp.bfloat16)
            out[pl.ds(dst, BLOCK), WIDTH:] = dv[j, pl.ds(src, BLOCK), :].astype(jnp.bfloat16)
            return 0
        lax.fori_loop(0, half_keys, give, 0, unroll=4)


def attend(q_rank, k_rank, q_sorted, k_sorted, counts, pays, kvs):
    key_blocks, query_blocks = k_rank.shape[0], q_rank.shape[0]
    keys = key_blocks * BLOCK
    key_tiles, query_tiles = keys // KEY_TILE, query_blocks // PAIR
    span = PAIR * COLS
    bf16, f32 = jnp.bfloat16, jnp.float32
    smem, vmem = pl.BlockSpec(memory_space=pltpu.SMEM), pl.BlockSpec(memory_space=pltpu.VMEM)
    listed = query_tiles * key_tiles + 2
    return pl.pallas_call(
        attend_kernel,
        in_specs=[smem] * 5 + [vmem] * 12,
        out_specs=[vmem] * 4,
        out_shape=[jax.ShapeDtypeStruct((8 * BLOCK, HALF_HEADS * WIDTH), bf16)] * 2
        + [jax.ShapeDtypeStruct((keys // 2, 2 * WIDTH), bf16)] * 2,
        scratch_shapes=[
            pltpu.VMEM((keys, WIDTH), bf16),
            pltpu.VMEM((keys, WIDTH), bf16),
            pltpu.VMEM((key_tiles, WIDTH, KEY_TILE), bf16),
            pltpu.VMEM((key_tiles, KEY_TILE, WIDTH), f32),
            pltpu.VMEM((key_tiles, KEY_TILE, WIDTH), f32),
            pltpu.VMEM((query_blocks * COLS, WIDTH), bf16),
            pltpu.VMEM((query_blocks * COLS, WIDTH), bf16),
            pltpu.VMEM((query_tiles, WIDTH, span), f32),
            pltpu.VMEM((query_blocks, COLS), f32),
            pltpu.VMEM((query_blocks, COLS), f32),
            pltpu.VMEM((2, KEY_TILE, span), f32),
            pltpu.VMEM((2, KEY_TILE, span), f32),
            pltpu.SMEM((2, listed), jnp.int32),
            pltpu.SMEM((2, listed), jnp.int32),
        ],
        compiler_params=pltpu.CompilerParams(vmem_limit_bytes=32 * 1024 * 1024),
    )(q_rank, k_rank, q_sorted, k_sorted, counts, *pays, *kvs)


def ranked(block_order, blocks):
    listed = jnp.arange(block_order.shape[0], dtype=jnp.int32)
    pos = jnp.sum(jnp.where(blocks[:, None] == listed[None, :], block_order[None, :], 0), axis=1)
    rank = jnp.sum((pos[None, :] < pos[:, None]).astype(jnp.int32), axis=1)
    at = jnp.arange(blocks.shape[0], dtype=jnp.int32)
    return rank, jnp.sum(jnp.where(rank[None, :] == at[:, None], pos[None, :], 0), axis=1)


def total_of(parts):
    return functools.reduce(lambda a, b: a + b, [p.astype(jnp.float32) for p in parts])


def thirds(array):
    high = lax.reduce_precision(array, 8, 7)
    middle = lax.reduce_precision(array - high, 8, 7)
    low = lax.reduce_precision(array - high - middle, 8, 7)
    return jnp.concatenate([high, middle, low], axis=1).astype(jnp.bfloat16)


def body(query_rows, key_rows, value_rows, saved_output, output_grad, logsumexp, block_order):
    rows = query_rows.shape[0]
    half = HALF_HEADS * WIDTH
    x, y, z, core = place(lax.axis_index("outer") * 8 + lax.axis_index("inner"))
    first = core == 0

    def mine(array):
        return jnp.where(first, array[:, :half], array[:, half:])

    def other(array):
        return jnp.where(first, array[:, half:], array[:, :half])

    heads = (rows, 2 * HALF_HEADS, WIDTH)
    delta = jnp.sum(
        output_grad.reshape(heads).astype(jnp.float32)
        * saved_output.reshape(heads).astype(jnp.float32), axis=2).T
    low = jnp.concatenate([logsumexp[:HALF_HEADS], delta[:HALF_HEADS]], axis=0)
    high = jnp.concatenate([logsumexp[HALF_HEADS:], delta[HALF_HEADS:]], axis=0)

    kv = jnp.concatenate([key_rows, value_rows], axis=1)
    sib = shift(jnp.concatenate([other(query_rows), other(output_grad)], axis=1), dcore=1)
    sib, kv = lax.optimization_barrier((sib, kv))
    stat_sib = shift(jnp.where(first, high, low), dcore=1)
    stat = thirds(jnp.concatenate([jnp.where(first, low, high), stat_sib], axis=0))
    stat = jnp.pad(stat, ((0, 0), (0, 2 * half - stat.shape[1])))
    pay = jnp.concatenate(
        [jnp.concatenate([mine(query_rows), mine(output_grad)], axis=1), stat, sib], axis=0)
    kv_line = jnp.concatenate([kv] + [shift(kv, dz=-d) for d in (1, 2, 3)], axis=0)
    lines = [kv_line] + [shift(kv_line, dx=-d) for d in (1, 2, 3)]
    after, before = shift(pay, dy=-1), shift(pay, dy=1)
    after, before, *lines = lax.optimization_barrier((after, before, *lines))
    across = shift(after[:SIB_AT], dy=-1), shift(before[SIB_AT:], dy=1)
    pays = [pay, after, *across, before]
    joined = [jnp.concatenate(lines[:2], axis=0), *lines[2:]]
    kvs = lines + [shift(line, dcore=1) for line in joined]

    four = jnp.arange(4, dtype=jnp.int32)
    two = jnp.arange(2, dtype=jnp.int32)
    dy, cs, b = (a.reshape(-1) for a in jnp.meshgrid(four, two, two, indexing="ij"))
    q_rank, q_sorted = ranked(block_order, 2 * linear(x, (y + dy) % 4, z, (core + cs) % 2) + b)
    cs, dx, dz, b = (a.reshape(-1) for a in jnp.meshgrid(two, four, four, two, indexing="ij"))
    k_rank, k_sorted = ranked(
        block_order, 2 * linear((x + dx) % 4, y, (z + dz) % 4, (core + cs) % 2) + b)

    tops, lows = q_sorted[PAIR - 1::PAIR], q_sorted[::PAIR]
    reached = jnp.sum((k_sorted[None, :] <= tops[:, None]).astype(jnp.int32), axis=1)
    passed = jnp.sum((k_sorted[None, :] < lows[:, None]).astype(jnp.int32), axis=1)
    per_tile = KEY_TILE // BLOCK
    counts = jnp.stack([passed // per_tile, (reached + per_tile - 1) // per_tile])

    dq_own, dq_sib, dkv_own, dkv_sib = attend(
        q_rank, k_rank, q_sorted, k_sorted, counts, pays, kvs)

    dkv = total_of([dkv_own, shift(dkv_sib, dcore=1)]).astype(jnp.bfloat16)
    dq_far = shift(dq_sib, dcore=1)
    dq = jnp.concatenate(
        [jnp.where(first, dq_own, dq_far), jnp.where(first, dq_far, dq_own)], axis=1)
    quarter = dkv.shape[0] // 4
    parts = [dkv[d * quarter:(d + 1) * quarter] for d in range(4)]
    line = total_of([parts[0]] + [shift(parts[d], dx=d) for d in (1, 2, 3)]).astype(jnp.bfloat16)
    parts = [line[d * rows:(d + 1) * rows] for d in range(4)]
    done = total_of([parts[0]] + [shift(parts[d], dz=d) for d in (1, 2, 3)])
    parts = [dq[d * rows:(d + 1) * rows] for d in range(4)]
    query_grad = total_of([parts[0]] + [shift(parts[d], dy=d) for d in (1, 2, 3)]).astype(jnp.bfloat16)
    return (
        query_grad,
        done[:, :WIDTH].astype(jnp.bfloat16),
        done[:, WIDTH:].astype(jnp.bfloat16),
    )


def solution(mesh):
    rows = P(AXES, None)
    return jax.shard_map(
        body,
        mesh=mesh,
        in_specs=(rows, rows, rows, rows, rows, P(None, AXES), P()),
        out_specs=(rows, rows, rows),
        check_vma=False,
    )
```

```python
import functools
import math

import jax
import jax.numpy as jnp
from jax import lax
from jax.experimental import pallas as pl
from jax.experimental.pallas import tpu as pltpu
from jax.sharding import PartitionSpec as P

WIDTH = 128
BLOCK = 64
KEY_TILE = 512
PAIR = 2
HALF_HEADS = 4
COLS = HALF_HEADS * BLOCK
STAT_ROWS = 16
SIB_AT = 2 * BLOCK + STAT_ROWS
LOG2E = 1.4426950408889634
AXES = ("outer", "inner")


def linear(x, y, z, core):
    return (((y % 2) * 4 + z) * 2 + core) * 8 + x * 2 + y // 2


def place(index):
    inner = index % 8
    outer = index // 8
    return inner // 2, (inner % 2) * 2 + outer // 8, (outer // 2) % 4, outer % 2


def shift(block, dx=0, dy=0, dz=0, dcore=0):
    route = []
    for index in range(128):
        x, y, z, core = place(index)
        to = linear((x + dx) % 4, (y + dy) % 4, (z + dz) % 4, (core + dcore) % 2)
        route.append((index, to))
    return lax.ppermute(block, AXES, route)


def nt(a, b):
    return lax.dot_general(a, b, (((1,), (1,)), ((), ())), preferred_element_type=jnp.float32)


def nn(a, b):
    return lax.dot_general(a, b, (((1,), (0,)), ((), ())), preferred_element_type=jnp.float32)


def attend_kernel(
    q_rank, k_rank, q_sorted, k_sorted, counts,
    pay0, pay1, pay2a, pay2b, pay3, own0, own1, own2, own3, sib0, sib1, sib2, sib3,
    dq_own, dq_sib, dkv_own, dkv_sib,
    ks, vs, kt, dk, dv, qs, gs, dq, lse_s, del_s, s_scr, p_scr, plain, edge,
):
    key_blocks, query_blocks = k_rank.shape[0], q_rank.shape[0]
    per_tile = KEY_TILE // BLOCK
    key_tiles, query_tiles = key_blocks // per_tile, query_blocks // PAIR
    half_keys = key_blocks // 2
    span = PAIR * COLS
    scale = 1.0 / math.sqrt(WIDTH)
    factor = scale * LOG2E

    for n, kv in enumerate((own0, own1, own2, own3, sib0, sib1, sib2, sib3)):
        def bring(r, _, kv=kv, n=n):
            src = pl.multiple_of(r * BLOCK, BLOCK)
            dst = pl.multiple_of(k_rank[n * 8 + r] * BLOCK, BLOCK)
            ks[pl.ds(dst, BLOCK), :] = kv[pl.ds(src, BLOCK), :WIDTH]
            vs[pl.ds(dst, BLOCK), :] = kv[pl.ds(src, BLOCK), WIDTH:]
            return 0
        lax.fori_loop(0, 8, bring, 0, unroll=4)

    def ready(j, _):
        kt[j] = ks[pl.ds(pl.multiple_of(j * KEY_TILE, KEY_TILE), KEY_TILE), :].T
        dk[j] = jnp.zeros((KEY_TILE, WIDTH), jnp.float32)
        dv[j] = jnp.zeros((KEY_TILE, WIDTH), jnp.float32)
        return 0
    lax.fori_loop(0, key_tiles, ready, 0)

    for s in range(query_blocks):
        pay, side = (pay0, pay1, pay2a, pay3)[s // 4], s % 4 // 2
        stats, rows = pay, side * SIB_AT + s % 2 * BLOCK
        if s // 4 == 2 and side:
            pay, rows = pay2b, s % 2 * BLOCK
        rank = q_rank[s]
        dst = pl.multiple_of(rank * COLS, COLS)
        for h in range(HALF_HEADS):
            qs[pl.ds(dst + h * BLOCK, BLOCK), :] = pay[rows:rows + BLOCK, h * WIDTH:(h + 1) * WIDTH]
            gs[pl.ds(dst + h * BLOCK, BLOCK), :] = pay[
                rows:rows + BLOCK, (HALF_HEADS + h) * WIDTH:(HALF_HEADS + h + 1) * WIDTH]
        stat = sum(
            stats[2 * BLOCK:SIB_AT, n * WIDTH:(n + 1) * WIDTH].astype(jnp.float32)
            for n in range(3))
        top, lanes = side * 2 * HALF_HEADS, slice(s % 2 * BLOCK, (s % 2 + 1) * BLOCK)
        lse_s[pl.ds(rank, 1), :] = jnp.concatenate(
            [stat[top + h:top + h + 1, lanes] for h in range(HALF_HEADS)], axis=1) * LOG2E
        top += HALF_HEADS
        del_s[pl.ds(rank, 1), :] = jnp.concatenate(
            [stat[top + h:top + h + 1, lanes] for h in range(HALF_HEADS)], axis=1)

    def listing(i, carry):
        dq[i] = jnp.zeros((WIDTH, span), jnp.float32)

        def put(listed):
            def one(j, at):
                listed[0, at] = i
                listed[1, at] = j
                return at + 1
            return one
        plains, edges = carry
        plains = lax.fori_loop(0, counts[0, i], put(plain), plains)
        return plains, lax.fori_loop(counts[0, i], counts[1, i], put(edge), edges)
    plains, edges = lax.fori_loop(0, query_tiles, listing, (jnp.int32(0), jnp.int32(0)))
    for listed, total in ((plain, plains), (edge, edges)):
        for extra in range(2):
            listed[0, total + extra] = 0
            listed[1, total + extra] = 0

    in_query = lax.broadcasted_iota(jnp.int32, (1, span), 1) % BLOCK
    in_key = lax.broadcasted_iota(jnp.int32, (BLOCK, span), 0)

    def sweep(listed, total, masked):
        def front(t, slot):
            i, j = listed[0, t], listed[1, t]
            ko, qo = pl.multiple_of(j * KEY_TILE, KEY_TILE), pl.multiple_of(i * span, span)
            s_scr[slot] = nt(ks[pl.ds(ko, KEY_TILE), :], qs[pl.ds(qo, span), :])
            p_scr[slot] = nt(vs[pl.ds(ko, KEY_TILE), :], gs[pl.ds(qo, span), :])

        def back(t, slot):
            i, j = listed[0, t], listed[1, t]
            qo = pl.multiple_of(i * span, span)
            lse = jnp.concatenate([lse_s[pl.ds(i * PAIR + u, 1), :] for u in range(PAIR)], axis=1)
            lse = jnp.where(t < total, lse, 1e30)
            delta = jnp.concatenate([del_s[pl.ds(i * PAIR + u, 1), :] for u in range(PAIR)], axis=1)
            query_pos = in_query + jnp.concatenate(
                [jnp.full((1, COLS), q_sorted[i * PAIR + u] * BLOCK, jnp.int32) for u in range(PAIR)],
                axis=1)
            probs_parts, dscores_parts = [], []
            for u in range(per_tile):
                scores = s_scr[slot, u * BLOCK:(u + 1) * BLOCK, :]
                dprobs = p_scr[slot, u * BLOCK:(u + 1) * BLOCK, :]
                probs = jnp.exp2(scores * factor - lse)
                if masked:
                    allowed = in_key <= query_pos - k_sorted[j * per_tile + u] * BLOCK
                    probs = jnp.where(allowed, probs, 0.0)
                dscores_parts.append((probs * (dprobs - delta)).astype(jnp.bfloat16))
                probs_parts.append(probs.astype(jnp.bfloat16))
            probs_half = jnp.concatenate(probs_parts, axis=0)
            dscores_half = jnp.concatenate(dscores_parts, axis=0)
            dv[j] += nn(probs_half, gs[pl.ds(qo, span), :])
            dk[j] += nn(dscores_half, qs[pl.ds(qo, span), :])
            dq[i] += nn(kt[j], dscores_half)

        front(0, 0)

        def two(h, _):
            front(2 * h + 1, 1)
            back(2 * h, 0)
            front(2 * h + 2, 0)
            back(2 * h + 1, 1)
            return 0
        lax.fori_loop(0, (total + 1) // 2, two, 0)

    sweep(plain, plains, False)
    sweep(edge, edges, True)

    for s in range(query_blocks):
        rank = q_rank[s]
        out = (dq_own, dq_sib)[s % 4 // 2]
        rows = s // 4 * 2 * BLOCK + s % 2 * BLOCK
        block = dq[rank // PAIR, :, pl.ds(pl.multiple_of(rank % PAIR * COLS, COLS), COLS)]
        block = (block.T * scale).astype(jnp.bfloat16)
        for h in range(HALF_HEADS):
            out[rows:rows + BLOCK, h * WIDTH:(h + 1) * WIDTH] = block[h * BLOCK:(h + 1) * BLOCK]
    for half, out in enumerate((dkv_own, dkv_sib)):
        def give(r, _, out=out, half=half):
            dst = pl.multiple_of(r * BLOCK, BLOCK)
            rank = k_rank[half * half_keys + r]
            j, src = rank // per_tile, pl.multiple_of(rank % per_tile * BLOCK, BLOCK)
            out[pl.ds(dst, BLOCK), :WIDTH] = (dk[j, pl.ds(src, BLOCK), :] * scale).astype(jnp.bfloat16)
            out[pl.ds(dst, BLOCK), WIDTH:] = dv[j, pl.ds(src, BLOCK), :].astype(jnp.bfloat16)
            return 0
        lax.fori_loop(0, half_keys, give, 0, unroll=4)


def attend(q_rank, k_rank, q_sorted, k_sorted, counts, pays, kvs):
    key_blocks, query_blocks = k_rank.shape[0], q_rank.shape[0]
    keys = key_blocks * BLOCK
    key_tiles, query_tiles = keys // KEY_TILE, query_blocks // PAIR
    span = PAIR * COLS
    bf16, f32 = jnp.bfloat16, jnp.float32
    smem, vmem = pl.BlockSpec(memory_space=pltpu.SMEM), pl.BlockSpec(memory_space=pltpu.VMEM)
    listed = query_tiles * key_tiles + 2
    return pl.pallas_call(
        attend_kernel,
        in_specs=[smem] * 5 + [vmem] * 13,
        out_specs=[vmem] * 4,
        out_shape=[jax.ShapeDtypeStruct((8 * BLOCK, HALF_HEADS * WIDTH), bf16)] * 2
        + [jax.ShapeDtypeStruct((keys // 2, 2 * WIDTH), bf16)] * 2,
        scratch_shapes=[
            pltpu.VMEM((keys, WIDTH), bf16),
            pltpu.VMEM((keys, WIDTH), bf16),
            pltpu.VMEM((key_tiles, WIDTH, KEY_TILE), bf16),
            pltpu.VMEM((key_tiles, KEY_TILE, WIDTH), f32),
            pltpu.VMEM((key_tiles, KEY_TILE, WIDTH), f32),
            pltpu.VMEM((query_blocks * COLS, WIDTH), bf16),
            pltpu.VMEM((query_blocks * COLS, WIDTH), bf16),
            pltpu.VMEM((query_tiles, WIDTH, span), f32),
            pltpu.VMEM((query_blocks, COLS), f32),
            pltpu.VMEM((query_blocks, COLS), f32),
            pltpu.VMEM((2, KEY_TILE, span), f32),
            pltpu.VMEM((2, KEY_TILE, span), f32),
            pltpu.SMEM((2, listed), jnp.int32),
            pltpu.SMEM((2, listed), jnp.int32),
        ],
        compiler_params=pltpu.CompilerParams(vmem_limit_bytes=32 * 1024 * 1024),
    )(q_rank, k_rank, q_sorted, k_sorted, counts, *pays, *kvs)


def ranked(block_order, blocks):
    listed = jnp.arange(block_order.shape[0], dtype=jnp.int32)
    pos = jnp.sum(jnp.where(blocks[:, None] == listed[None, :], block_order[None, :], 0), axis=1)
    rank = jnp.sum((pos[None, :] < pos[:, None]).astype(jnp.int32), axis=1)
    at = jnp.arange(blocks.shape[0], dtype=jnp.int32)
    return rank, jnp.sum(jnp.where(rank[None, :] == at[:, None], pos[None, :], 0), axis=1)


def total_of(parts):
    return functools.reduce(lambda a, b: a + b, [p.astype(jnp.float32) for p in parts])


def thirds(array):
    high = lax.reduce_precision(array, 8, 7)
    middle = lax.reduce_precision(array - high, 8, 7)
    low = lax.reduce_precision(array - high - middle, 8, 7)
    return jnp.concatenate([high, middle, low], axis=1).astype(jnp.bfloat16)


def body(query_rows, key_rows, value_rows, saved_output, output_grad, logsumexp, block_order):
    rows = query_rows.shape[0]
    half = HALF_HEADS * WIDTH
    x, y, z, core = place(lax.axis_index("outer") * 8 + lax.axis_index("inner"))
    first = core == 0

    def mine(array):
        return jnp.where(first, array[:, :half], array[:, half:])

    def other(array):
        return jnp.where(first, array[:, half:], array[:, :half])

    heads = (rows, 2 * HALF_HEADS, WIDTH)
    delta = jnp.sum(
        output_grad.reshape(heads).astype(jnp.float32)
        * saved_output.reshape(heads).astype(jnp.float32), axis=2).T
    low = jnp.concatenate([logsumexp[:HALF_HEADS], delta[:HALF_HEADS]], axis=0)
    high = jnp.concatenate([logsumexp[HALF_HEADS:], delta[HALF_HEADS:]], axis=0)

    kv = jnp.concatenate([key_rows, value_rows], axis=1)
    sib = shift(jnp.concatenate([other(query_rows), other(output_grad)], axis=1), dcore=1)
    sib, kv = lax.optimization_barrier((sib, kv))
    stat_sib = shift(jnp.where(first, high, low), dcore=1)
    stat = thirds(jnp.concatenate([jnp.where(first, low, high), stat_sib], axis=0))
    stat = jnp.pad(stat, ((0, 0), (0, 2 * half - stat.shape[1])))
    pay = jnp.concatenate(
        [jnp.concatenate([mine(query_rows), mine(output_grad)], axis=1), stat, sib], axis=0)
    kv_line = jnp.concatenate([kv] + [shift(kv, dz=-d) for d in (1, 2, 3)], axis=0)
    after, before = shift(pay, dy=-1), shift(pay, dy=1)
    right, left, line_sib = shift(kv_line, dx=-1), shift(kv_line, dx=1), shift(kv_line, dcore=1)
    after, before, kv_line, line_sib, right, left = lax.optimization_barrier(
        (after, before, kv_line, line_sib, right, left))
    across = shift(after[:SIB_AT], dy=-1), shift(before[SIB_AT:], dy=1)
    beyond = shift(kv_line, dx=2)
    pays = [pay, after, *across, before]
    kvs = [kv_line, right, beyond, left, line_sib]
    kvs += [shift(line, dcore=1) for line in (right, beyond, left)]

    four = jnp.arange(4, dtype=jnp.int32)
    two = jnp.arange(2, dtype=jnp.int32)
    dy, cs, b = (a.reshape(-1) for a in jnp.meshgrid(four, two, two, indexing="ij"))
    q_rank, q_sorted = ranked(block_order, 2 * linear(x, (y + dy) % 4, z, (core + cs) % 2) + b)
    cs, dx, dz, b = (a.reshape(-1) for a in jnp.meshgrid(two, four, four, two, indexing="ij"))
    k_rank, k_sorted = ranked(
        block_order, 2 * linear((x + dx) % 4, y, (z + dz) % 4, (core + cs) % 2) + b)

    tops, lows = q_sorted[PAIR - 1::PAIR], q_sorted[::PAIR]
    reached = jnp.sum((k_sorted[None, :] <= tops[:, None]).astype(jnp.int32), axis=1)
    passed = jnp.sum((k_sorted[None, :] < lows[:, None]).astype(jnp.int32), axis=1)
    per_tile = KEY_TILE // BLOCK
    counts = jnp.stack([passed // per_tile, (reached + per_tile - 1) // per_tile])

    dq_own, dq_sib, dkv_own, dkv_sib = attend(
        q_rank, k_rank, q_sorted, k_sorted, counts, pays, kvs)

    dkv = total_of([dkv_own, shift(dkv_sib, dcore=1)]).astype(jnp.bfloat16)
    dq_far = shift(dq_sib, dcore=1)
    dq = jnp.concatenate(
        [jnp.where(first, dq_own, dq_far), jnp.where(first, dq_far, dq_own)], axis=1)
    quarter = dkv.shape[0] // 4
    parts = [dkv[d * quarter:(d + 1) * quarter] for d in range(4)]
    line = total_of([parts[0]] + [shift(parts[d], dx=d) for d in (1, 2, 3)]).astype(jnp.bfloat16)
    parts = [line[d * rows:(d + 1) * rows] for d in range(4)]
    done = total_of([parts[0]] + [shift(parts[d], dz=d) for d in (1, 2, 3)])
    parts = [dq[d * rows:(d + 1) * rows] for d in range(4)]
    query_grad = total_of([parts[0]] + [shift(parts[d], dy=d) for d in (1, 2, 3)]).astype(jnp.bfloat16)
    return (
        query_grad,
        done[:, :WIDTH].astype(jnp.bfloat16),
        done[:, WIDTH:].astype(jnp.bfloat16),
    )


def solution(mesh):
    rows = P(AXES, None)
    return jax.shard_map(
        body,
        mesh=mesh,
        in_specs=(rows, rows, rows, rows, rows, P(None, AXES), P()),
        out_specs=(rows, rows, rows),
        check_vma=False,
    )
```
